32 devices in a mesh: groups: 2 (over x), cols: 16 (over z, y, core).
Axes of the slice: x: 2, y: 2, z: 4, core: 2. Of those that a mesh axis runs over, the one named last changes fastest.
Arguments:
- upper_left: bfloat16 [76800, 1024], P(('groups', 'cols')), parts along dimension 0, may hold values from -0.25 to 0.25
- upper_right: bfloat16 [76800, 1024], P(('groups', 'cols')), parts along dimension 0, may hold values from -0.0390625 to 0.0390625
- lower_left: bfloat16 [76800, 1024], P(('groups', 'cols')), parts along dimension 0, may hold values from -0.0390625 to 0.0390625
- lower_right: bfloat16 [76800, 1024], P(('groups', 'cols')), parts along dimension 0, may hold values from -0.25 to 0.25
- sketch_right: bfloat16 [76800, 384], P(('groups', 'cols')), parts along dimension 0, may hold values from -6 to 6
- sketch_left: bfloat16 [76800, 384], P(('groups', 'cols')), parts along dimension 0, may hold values from -6 to 6
- pairing: int32 [32], P('groups'), parts along dimension 0, may hold values from 0 to 15, each once
Outputs:
- upper_panel: float32 [2048, 384], P(('groups', 'cols')), parts along dimension 0
- lower_panel: float32 [2048, 384], P(('groups', 'cols')), parts along dimension 0
The draws below stay inside these ranges and needn't reach their ends.
There are 2 independent parts, one for each index of `groups`. The reference program is written for one: setup_inputs(seed, part) draws one part's arguments, and reference() takes and returns one part's arrays. A program takes and returns all parts, laid end to end along the dimension named above; each array names one. Nothing has to cross between parts.
Inputs may be any that keep to these rules, and one draw needn't show every extreme that they name: pairing names every index of the cols axis once.
All inputs are finite; a program needn't handle non-finite values.
Results may differ from the reference program's by a relative error of at most 0.0089.
Values may be sent and summed in bfloat16 or wider, within the bound.
A program may use at most 128 MiB of HBM per device.

```python
import jax
import jax.numpy as jnp
from jax import lax

CHI = 384
PANEL = 1024
HALF = 38400
N_COLS = 16


def spiked(array, rng, source, target, blocks, factor):
    def block_of(position):
        return (jnp.arange(array.shape[position]) // (array.shape[position] // blocks)).reshape((-1,) + (1,) * (array.ndim - 1 - position))

    one_side = jax.random.permutation(rng, blocks)[block_of(target)]
    second = (block_of(target) + blocks // 2) % blocks
    return jnp.where((block_of(source) == one_side) | (block_of(source) == second), factor * array, array)


def levels(key, extent, pieces, smallest, top_value):
    factor_of = 1.0
    for position, parts in pieces:
        steps = jax.random.uniform(jax.random.fold_in(jax.random.fold_in(key, 6), position), (parts,), jnp.float32, smallest / len(pieces), top_value / len(pieces))
        factor_of = factor_of * jnp.repeat(jnp.exp(steps), extent[position] // parts).reshape((-1,) + (1,) * (len(extent) - 1 - position))
    return factor_of


def normal_values(rng, extent, scale, limit, cuts=(), held_as=jnp.bfloat16):
    loudness = levels(rng, extent, cuts, -0.22, 0.18) if cuts else 1.0
    values = jax.random.normal(rng, extent, jnp.float32) * scale * loudness
    return jnp.minimum(jnp.maximum(values, -limit), limit).astype(held_as)


def heavy_noise(rng, extent, deviation, reach, cuts, heavy, kind=jnp.bfloat16):
    values = deviation * jax.random.normal(rng, extent, jnp.float32)
    if cuts:
        values = values * levels(rng, extent, cuts, -0.22, 0.18)
    return jnp.clip(spiked(values, jax.random.fold_in(rng, 3), *heavy), -reach, reach).astype(kind)


def setup_inputs(seed: int = 0, part: int = 0) -> dict:
    streams_of = jax.random.split(jax.random.key(seed), 8)
    own_keys = jax.random.split(jax.random.fold_in(streams_of[7], part), 8)
    return {
        "upper_left": heavy_noise(own_keys[0], (HALF, PANEL), PANEL ** -0.5, 0.25, ((0, 16),), (0, 1, 16, 2.0)),
        "upper_right": heavy_noise(own_keys[1], (HALF, PANEL), HALF ** -0.5, 0.0390625, ((0, 16),), (0, 1, 16, 2.0)),
        "lower_left": heavy_noise(own_keys[2], (HALF, PANEL), HALF ** -0.5, 0.0390625, ((0, 16),), (0, 1, 16, 2.0)),
        "lower_right": heavy_noise(own_keys[3], (HALF, PANEL), PANEL ** -0.5, 0.25, ((0, 16),), (0, 1, 16, 2.0)),
        "sketch_right": normal_values(own_keys[4], (HALF, CHI), 1.0, 6.0, ((0, 16),)),
        "sketch_left": normal_values(own_keys[5], (HALF, CHI), 1.0, 6.0, ((0, 16),)),
        "pairing": jax.random.permutation(own_keys[6], N_COLS).astype(jnp.int32),
    }


def contract(first, second):
    return lax.dot_general(first.astype(jnp.float32), second.astype(jnp.float32), (((0,), (0,)), ((), ())), preferred_element_type=jnp.float32)

def contract_exact(first, second):
    return lax.dot_general(first.astype(jnp.float32), second.astype(jnp.float32), (((0,), (0,)), ((), ())), precision=lax.Precision.HIGHEST, preferred_element_type=jnp.float32)

def orthonormal(range_mat):
    gram = contract_exact(range_mat, range_mat) / range_mat.shape[0]
    factor = jnp.linalg.cholesky(gram)
    return lax.linalg.triangular_solve(factor, range_mat, left_side=False, lower=True, transpose_a=True)

def reference(upper_left, upper_right, lower_left, lower_right, sketch_right, sketch_left, pairing):
    block_rows = PANEL // N_COLS
    columns = jnp.arange(PANEL, dtype=jnp.int32)
    column_map = (pairing[columns // block_rows] * block_rows + columns % block_rows).astype(jnp.int32)
    aligned = jnp.take(lower_right, column_map, axis=1)
    first_right = contract(lower_left, sketch_right).astype(jnp.bfloat16)
    first_left = contract(upper_left, sketch_left).astype(jnp.bfloat16)
    second_right = jnp.dot(aligned.astype(jnp.float32), first_right.astype(jnp.float32), preferred_element_type=jnp.float32).astype(jnp.bfloat16)
    second_left = jnp.dot(upper_right.astype(jnp.float32), first_left.astype(jnp.float32), preferred_element_type=jnp.float32).astype(jnp.bfloat16)
    third_right = contract(upper_right, second_right).astype(jnp.bfloat16)
    third_left = contract(aligned, second_left).astype(jnp.bfloat16)
    range_right = jnp.dot(upper_left.astype(jnp.float32), third_right.astype(jnp.float32), preferred_element_type=jnp.float32)
    range_left = jnp.dot(lower_left.astype(jnp.float32), third_left.astype(jnp.float32), preferred_element_type=jnp.float32)
    basis_right = orthonormal(range_right)
    basis_left = orthonormal(range_left)
    upper_panel = contract_exact(upper_left.astype(jnp.float32), basis_right)
    lower_panel = contract_exact(lower_left.astype(jnp.float32), basis_left)
    return (upper_panel, lower_panel)
```

```python
import functools

import jax
import jax.numpy as jnp
from jax import lax
from jax.experimental import pallas as pl
from jax.experimental.pallas import tpu as pltpu
from jax.sharding import PartitionSpec as P

BLOCK = 256
PIVOTS = 64
F32 = jnp.float32
BF16 = jnp.bfloat16


def contract(first, second):
    return lax.dot_general(
        first, second, (((0,), (0,)), ((), ())), preferred_element_type=F32
    )


def dot_exact(first, second, dims=((1,), (0,))):
    return lax.dot_general(
        first, second, (dims, ((), ())), precision=lax.Precision.HIGHEST, preferred_element_type=F32
    )


def upper_blocks(array):
    order = array.shape[1]
    return jnp.concatenate(
        [contract(array[:, k : k + BLOCK], array[:, k:]) for k in range(0, order, BLOCK)], axis=1
    )


def exchange(value, bit, count):
    return lax.ppermute(value, "cols", [(i, i ^ (1 << bit)) for i in range(count)])


def sum_rows(partial, bits, me, count):
    for bit in bits:
        half = partial.shape[0] // 2
        mine = (me >> bit) & 1
        kept = lax.dynamic_slice_in_dim(partial, mine * half, half, 0)
        sent = lax.dynamic_slice_in_dim(partial, (1 - mine) * half, half, 0).astype(BF16)
        partial = kept + exchange(sent, bit, count).astype(F32)
    share = partial.astype(BF16)
    for bit in reversed(bits):
        mine = (me >> bit) & 1
        other = exchange(share, bit, count)
        share = jnp.where(
            mine == 0,
            jnp.concatenate([share, other], axis=0),
            jnp.concatenate([other, share], axis=0),
        )
    return share


def inverse_factors(blocks):
    size = PIVOTS
    rows = size // 8
    eye = (
        lax.broadcasted_iota(jnp.int32, (size, size), 0)
        == lax.broadcasted_iota(jnp.int32, (size, size), 1)
    ).astype(F32)
    sub = lax.broadcasted_iota(jnp.int32, (8, 2 * size), 0)
    tables = []
    for block in blocks:
        joined = jnp.concatenate([block, eye], axis=1)
        tables.append([joined[8 * c : 8 * c + 8] for c in range(rows)])
    for j in range(size):
        c0, r0 = j // 8, j % 8
        for t in tables:
            row = jnp.broadcast_to(t[c0][r0 : r0 + 1, :], (8, 2 * size))
            inv = 1.0 / jnp.broadcast_to(row[:, j : j + 1], (8, 2 * size))
            scaled = row * inv
            for c in range(c0, rows):
                col = jnp.broadcast_to(t[c][:, j : j + 1], (8, 2 * size))
                if c == c0:
                    col = jnp.where(sub > r0, col, 0.0)
                t[c] = t[c] - col * scaled
    out = []
    for t in tables:
        joined = jnp.concatenate(t, axis=0)
        diag = jnp.sum(joined[:, :size] * eye, axis=1, keepdims=True)
        out.append(joined[:, size:] * lax.rsqrt(diag))
    return out


def split3(value):
    high = value.astype(BF16)
    rest = value - high.astype(F32)
    mid = rest.astype(BF16)
    return high, mid, (rest - mid.astype(F32)).astype(BF16)


def tail_kernel(
    where_ref, pairing_ref, first_ref, middle_ref, upper_ref, lower_ref,
    out_up, out_low, moved, loose, gram_ref, table, *, half_rows, units
):
    order, rank2 = first_ref.shape
    rank = rank2 // 2
    unit = order // units
    share = out_up.shape[0]

    loose[...] = first_ref[:, :rank].astype(F32)

    @pl.loop(0, units)
    def _(i):
        moved[pl.ds(pl.multiple_of(pairing_ref[i] * unit, unit), unit), :] = loose[
            pl.ds(pl.multiple_of(i * unit, unit), unit), :
        ]

    third_right = jnp.dot(middle_ref[...], moved[...].astype(BF16), preferred_element_type=F32).astype(BF16)
    loose[...] = lax.dot_general(
        middle_ref[...], first_ref[:, rank:], (((0,), (0,)), ((), ())), preferred_element_type=F32
    )

    @pl.loop(0, units)
    def _(i):
        moved[pl.ds(pl.multiple_of(i * unit, unit), unit), :] = loose[
            pl.ds(pl.multiple_of(pairing_ref[i] * unit, unit), unit), :
        ]

    thirds = (third_right, moved[...].astype(BF16))
    for s, (third, square_ref) in enumerate(zip(thirds, (upper_ref, lower_ref))):
        base = 0
        parts = [None] * (order // BLOCK)
        for k in range(order // BLOCK):
            width = order - k * BLOCK
            strip = square_ref[:, base : base + width]
            base += width
            term = jnp.dot(strip, third[k * BLOCK :], preferred_element_type=F32)
            parts[k] = term if parts[k] is None else parts[k] + term
            if width > BLOCK:
                below = lax.dot_general(
                    strip[:, BLOCK:],
                    third[k * BLOCK : (k + 1) * BLOCK],
                    (((0,), (0,)), ((), ())),
                    preferred_element_type=F32,
                )
                for m in range(k + 1, order // BLOCK):
                    piece = below[(m - k - 1) * BLOCK : (m - k) * BLOCK]
                    parts[m] = piece if parts[m] is None else parts[m] + piece
        for k in range(order // BLOCK):
            table[s, k * BLOCK : (k + 1) * BLOCK, :] = parts[k]
        product = table[s]
        gram = sum(contract(third, piece) for piece in split3(product)) * (1.0 / half_rows)
        gram_ref[s, :, :rank] = gram
        gram_ref[s, :, rank:] = (
            lax.broadcasted_iota(jnp.int32, (rank, rank), 0)
            == lax.broadcasted_iota(jnp.int32, (rank, rank), 1)
        ).astype(F32)

    @pl.loop(0, rank // PIVOTS)
    def _(k):
        at = pl.multiple_of(k * PIVOTS, PIVOTS)
        rows = [gram_ref[s, pl.ds(at, PIVOTS), :] for s in range(2)]
        turned = [pltpu.roll(r[:, :rank], rank - at, 1)[:, :PIVOTS] for r in rows]
        inverses = inverse_factors(turned)
        beyond = lax.broadcasted_iota(jnp.int32, (PIVOTS, rank), 1) >= at + PIVOTS
        for s in range(2):
            done = dot_exact(inverses[s], rows[s])
            ahead = jnp.where(beyond, done[:, :rank], 0.0)
            gram_ref[s, :, :] = gram_ref[s, :, :] - dot_exact(ahead, done, ((0,), (0,)))
            gram_ref[s, pl.ds(at, PIVOTS), :] = done

    at = pl.multiple_of(where_ref[0] * share, share)
    for s, out in enumerate((out_up, out_low)):
        out[...] = dot_exact(
            table[s, pl.ds(at, share), :], gram_ref[s, :, rank:], ((1,), (1,))
        )


def tail(me, pairing, first, middle, upper, lower, half_rows, count):
    order = first.shape[0]
    rank = first.shape[1] // 2
    share = jax.ShapeDtypeStruct((order // count, rank), F32)
    smem = pl.BlockSpec(memory_space=pltpu.SMEM)
    vmem = pl.BlockSpec(memory_space=pltpu.VMEM)
    return pl.pallas_call(
        functools.partial(tail_kernel, half_rows=half_rows, units=count),
        out_shape=(share, share),
        in_specs=[smem, smem, vmem, vmem, vmem, vmem],
        out_specs=(vmem, vmem),
        scratch_shapes=[
            pltpu.VMEM((order, rank), F32),
            pltpu.VMEM((order, rank), F32),
            pltpu.VMEM((2, rank, 2 * rank), F32),
            pltpu.VMEM((2, order, rank), F32),
        ],
        compiler_params=pltpu.CompilerParams(vmem_limit_bytes=48 * 2**20),
    )(me[None], pairing, first, middle, upper, lower)


def per_device(
    upper_left, upper_right, lower_left, lower_right, sketch_right, sketch_left, pairing
):
    count = lax.axis_size("cols")
    me = lax.axis_index("cols").astype(jnp.int32)
    half_rows = upper_left.shape[0] * count
    bits = list(range(count.bit_length() - 1))
    near_first = bits
    far_first = bits[:1] + bits[2:] + bits[1:2]
    middle = sum_rows(contract(upper_right, lower_right), near_first, me, count)
    first = sum_rows(
        jnp.concatenate(
            [contract(lower_left, sketch_right), contract(upper_left, sketch_left)], axis=1
        ),
        far_first, me, count,
    )
    upper = sum_rows(upper_blocks(upper_left), near_first, me, count)
    lower = sum_rows(upper_blocks(lower_left), far_first, me, count)
    return tail(me, pairing, first, middle, upper, lower, half_rows, count)


def solution(mesh):
    rows = P(("groups", "cols"), None)
    return jax.shard_map(
        per_device,
        mesh=mesh,
        in_specs=(rows,) * 6 + (P("groups"),),
        out_specs=(rows, rows),
        check_vma=False,
    )
```

```python
import functools

import jax
import jax.numpy as jnp
from jax import lax
from jax.experimental import pallas as pl
from jax.experimental.pallas import tpu as pltpu
from jax.sharding import PartitionSpec as P

BLOCK = 256
PIVOTS = 64
F32 = jnp.float32
BF16 = jnp.bfloat16


def contract(first, second):
    return lax.dot_general(
        first, second, (((0,), (0,)), ((), ())), preferred_element_type=F32
    )


def dot_exact(first, second, dims=((1,), (0,))):
    return lax.dot_general(
        first, second, (dims, ((), ())), precision=lax.Precision.HIGHEST, preferred_element_type=F32
    )


def strips(first, second):
    return [
        contract(first[:, k : k + BLOCK], second) for k in range(0, first.shape[1], BLOCK)
    ]


def upper_strips(array):
    return [
        contract(array[:, k : k + BLOCK], array[:, k:]) for k in range(0, array.shape[1], BLOCK)
    ]


def exchange(value, bit, count):
    return lax.ppermute(value, "cols", [(i, i ^ (1 << bit)) for i in range(count)])


def sum_rows(partial, bits, me, count):
    for bit in bits:
        half = partial.shape[0] // 2
        mine = (me >> bit) & 1
        kept = lax.dynamic_slice_in_dim(partial, mine * half, half, 0)
        sent = lax.dynamic_slice_in_dim(partial, (1 - mine) * half, half, 0).astype(BF16)
        partial = kept + exchange(sent, bit, count).astype(F32)
    share = partial.astype(BF16)
    for bit in reversed(bits):
        mine = (me >> bit) & 1
        other = exchange(share, bit, count)
        share = jnp.where(
            mine == 0,
            jnp.concatenate([share, other], axis=0),
            jnp.concatenate([other, share], axis=0),
        )
    return share


def inverse_factors(blocks):
    size = PIVOTS
    rows = size // 8
    eye = (
        lax.broadcasted_iota(jnp.int32, (size, size), 0)
        == lax.broadcasted_iota(jnp.int32, (size, size), 1)
    ).astype(F32)
    sub = lax.broadcasted_iota(jnp.int32, (8, 2 * size), 0)
    tables = []
    for block in blocks:
        joined = jnp.concatenate([block, eye], axis=1)
        tables.append([joined[8 * c : 8 * c + 8] for c in range(rows)])
    wide = (8, 2 * size)
    for j in range(0, size, 2):
        c0, r0 = j // 8, j % 8
        for t in tables:
            head = t[c0]
            row0 = jnp.broadcast_to(head[r0 : r0 + 1, :], wide)
            row1 = jnp.broadcast_to(head[r0 + 1 : r0 + 2, :], wide)
            a = jnp.broadcast_to(row0[:, j : j + 1], wide)
            b = jnp.broadcast_to(row1[:, j : j + 1], wide)
            c = jnp.broadcast_to(row1[:, j + 1 : j + 2], wide)
            inv = 1.0 / a
            ratio = b * inv
            inv1 = 1.0 / (c - ratio * b)
            lifted = row1 - ratio * row0
            scaled0 = row0 * inv
            scaled1 = lifted * inv1
            for k in range(c0, rows):
                col0 = jnp.broadcast_to(t[k][:, j : j + 1], wide)
                col1 = jnp.broadcast_to(t[k][:, j + 1 : j + 2], wide) - ratio * col0
                if k == c0:
                    col0 = jnp.where(sub > r0, col0, 0.0)
                    col1 = jnp.where(sub > r0 + 1, col1, 0.0)
                t[k] = t[k] - col0 * scaled0 - col1 * scaled1
    out = []
    for t in tables:
        joined = jnp.concatenate(t, axis=0)
        diag = jnp.sum(joined[:, :size] * eye, axis=1, keepdims=True)
        out.append(joined[:, size:] * lax.rsqrt(diag))
    return out


def split3(value):
    high = value.astype(BF16)
    rest = value - high.astype(F32)
    mid = rest.astype(BF16)
    return high, mid, (rest - mid.astype(F32)).astype(BF16)


def tail_kernel(
    where_ref, pairing_ref, near_ref, far_ref,
    out_up, out_low, moved, loose, gram_ref, table, *, half_rows, units
):
    order, rank = moved.shape
    sides = order // BLOCK
    unit = order // units
    share = out_up.shape[0]

    for k in range(sides):
        loose[k * BLOCK : (k + 1) * BLOCK, :] = far_ref[:, k * rank : (k + 1) * rank].astype(F32)

    @pl.loop(0, units)
    def _(i):
        moved[pl.ds(pl.multiple_of(pairing_ref[i] * unit, unit), unit), :] = loose[
            pl.ds(pl.multiple_of(i * unit, unit), unit), :
        ]

    swapped = moved[...].astype(BF16)
    third_right = jnp.concatenate(
        [
            jnp.dot(
                near_ref[:, k * order : (k + 1) * order], swapped, preferred_element_type=F32
            ).astype(BF16)
            for k in range(sides)
        ],
        axis=0,
    )
    left = sides * rank
    loose[...] = sum(
        contract(
            near_ref[:, k * order : (k + 1) * order],
            far_ref[:, left + k * rank : left + (k + 1) * rank],
        )
        for k in range(sides)
    )

    @pl.loop(0, units)
    def _(i):
        moved[pl.ds(pl.multiple_of(i * unit, unit), unit), :] = loose[
            pl.ds(pl.multiple_of(pairing_ref[i] * unit, unit), unit), :
        ]

    thirds = (third_right, moved[...].astype(BF16))
    for s, (third, square_ref) in enumerate(zip(thirds, (near_ref, far_ref))):
        base = (sides * order, 2 * left)[s]
        parts = [None] * (order // BLOCK)
        for k in range(order // BLOCK):
            width = order - k * BLOCK
            strip = square_ref[:, base : base + width]
            base += width
            term = jnp.dot(strip, third[k * BLOCK :], preferred_element_type=F32)
            parts[k] = term if parts[k] is None else parts[k] + term
            if width > BLOCK:
                below = lax.dot_general(
                    strip[:, BLOCK:],
                    third[k * BLOCK : (k + 1) * BLOCK],
                    (((0,), (0,)), ((), ())),
                    preferred_element_type=F32,
                )
                for m in range(k + 1, order // BLOCK):
                    piece = below[(m - k - 1) * BLOCK : (m - k) * BLOCK]
                    parts[m] = piece if parts[m] is None else parts[m] + piece
        for k in range(order // BLOCK):
            table[s, k * BLOCK : (k + 1) * BLOCK, :] = parts[k]
        product = table[s]
        gram = sum(contract(third, piece) for piece in split3(product)) * (1.0 / half_rows)
        gram_ref[s, :, :rank] = gram
        gram_ref[s, :, rank:] = (
            lax.broadcasted_iota(jnp.int32, (rank, rank), 0)
            == lax.broadcasted_iota(jnp.int32, (rank, rank), 1)
        ).astype(F32)

    @pl.loop(0, rank // PIVOTS)
    def _(k):
        at = pl.multiple_of(k * PIVOTS, PIVOTS)
        rows = [gram_ref[s, pl.ds(at, PIVOTS), :] for s in range(2)]
        turned = [pltpu.roll(r[:, :rank], rank - at, 1)[:, :PIVOTS] for r in rows]
        inverses = inverse_factors(turned)
        beyond = lax.broadcasted_iota(jnp.int32, (PIVOTS, rank), 1) >= at + PIVOTS
        for s in range(2):
            done = dot_exact(inverses[s], rows[s])
            ahead = jnp.where(beyond, done[:, :rank], 0.0)
            gram_ref[s, :, :] = gram_ref[s, :, :] - dot_exact(ahead, done, ((0,), (0,)))
            gram_ref[s, pl.ds(at, PIVOTS), :] = done

    at = pl.multiple_of(where_ref[0] * share, share)
    for s, out in enumerate((out_up, out_low)):
        out[...] = dot_exact(
            table[s, pl.ds(at, share), :], gram_ref[s, :, rank:], ((1,), (1,))
        )


def tail(me, pairing, near, far, order, rank, half_rows, count):
    share = jax.ShapeDtypeStruct((order // count, rank), F32)
    smem = pl.BlockSpec(memory_space=pltpu.SMEM)
    vmem = pl.BlockSpec(memory_space=pltpu.VMEM)
    return pl.pallas_call(
        functools.partial(tail_kernel, half_rows=half_rows, units=count),
        out_shape=(share, share),
        in_specs=[smem, smem, vmem, vmem],
        out_specs=(vmem, vmem),
        scratch_shapes=[
            pltpu.VMEM((order, rank), F32),
            pltpu.VMEM((order, rank), F32),
            pltpu.VMEM((2, rank, 2 * rank), F32),
            pltpu.VMEM((2, order, rank), F32),
        ],
        compiler_params=pltpu.CompilerParams(vmem_limit_bytes=48 * 2**20),
    )(me[None], pairing, near, far)


def per_device(
    upper_left, upper_right, lower_left, lower_right, sketch_right, sketch_left, pairing
):
    count = lax.axis_size("cols")
    me = lax.axis_index("cols").astype(jnp.int32)
    half_rows = upper_left.shape[0] * count
    order, rank = upper_left.shape[1], sketch_right.shape[1]
    bits = list(range(count.bit_length() - 1))
    near_first = bits
    far_first = bits[:1] + bits[2:] + bits[1:2]
    near = sum_rows(
        jnp.concatenate(strips(upper_right, lower_right) + upper_strips(upper_left), axis=1),
        near_first, me, count,
    )
    far = sum_rows(
        jnp.concatenate(
            strips(lower_left, sketch_right)
            + strips(upper_left, sketch_left)
            + upper_strips(lower_left),
            axis=1,
        ),
        far_first, me, count,
    )
    return tail(me, pairing, near, far, order, rank, half_rows, count)


def solution(mesh):
    rows = P(("groups", "cols"), None)
    return jax.shard_map(
        per_device,
        mesh=mesh,
        in_specs=(rows,) * 6 + (P("groups"),),
        out_specs=(rows, rows),
        check_vma=False,
    )
```

```python
import functools

import jax
import jax.numpy as jnp
from jax import lax
from jax.experimental import pallas as pl
from jax.experimental.pallas import tpu as pltpu
from jax.sharding import PartitionSpec as P

BLOCK = 256
PIVOTS = 64
F32 = jnp.float32
BF16 = jnp.bfloat16


def contract(first, second):
    return lax.dot_general(
        first, second, (((0,), (0,)), ((), ())), preferred_element_type=F32
    )


def dot_exact(first, second, dims=((1,), (0,))):
    return lax.dot_general(
        first, second, (dims, ((), ())), precision=lax.Precision.HIGHEST, preferred_element_type=F32
    )


def strips(first, second):
    return [
        contract(first[:, k : k + BLOCK], second) for k in range(0, first.shape[1], BLOCK)
    ]


def upper_strips(array):
    return [
        contract(array[:, k : k + BLOCK], array[:, k:]) for k in range(0, array.shape[1], BLOCK)
    ]


def exchange(value, bit, count):
    return lax.ppermute(value, "cols", [(i, i ^ (1 << bit)) for i in range(count)])


def exchange_all(values, bits, count, together):
    if together:
        values = lax.optimization_barrier(tuple(values))
    return tuple(exchange(value, bit, count) for value, bit in zip(values, bits))


def sum_rows(partials, orders, me, count):
    for stage, bits in enumerate(zip(*orders)):
        kept, sent = [], []
        for partial, bit in zip(partials, bits):
            half = partial.shape[0] // 2
            mine = (me >> bit) & 1
            kept.append(lax.dynamic_slice_in_dim(partial, mine * half, half, 0))
            sent.append(
                lax.dynamic_slice_in_dim(partial, (1 - mine) * half, half, 0).astype(BF16)
            )
        others = exchange_all(sent, bits, count, stage == 1)
        partials = [k + other.astype(F32) for k, other in zip(kept, others)]
    shares = [partial.astype(BF16) for partial in partials]
    for bits in reversed(list(zip(*orders))):
        others = exchange_all(shares, bits, count, False)
        shares = [
            jnp.where(
                (me >> bit) & 1 == 0,
                jnp.concatenate([share, other], axis=0),
                jnp.concatenate([other, share], axis=0),
            )
            for share, other, bit in zip(shares, others, bits)
        ]
    return shares


def inverse_factors(blocks):
    size = PIVOTS
    rows = size // 8
    eye = (
        lax.broadcasted_iota(jnp.int32, (size, size), 0)
        == lax.broadcasted_iota(jnp.int32, (size, size), 1)
    ).astype(F32)
    sub = lax.broadcasted_iota(jnp.int32, (8, 2 * size), 0)
    tables = []
    for block in blocks:
        joined = jnp.concatenate([block, eye], axis=1)
        tables.append([joined[8 * c : 8 * c + 8] for c in range(rows)])
    wide = (8, 2 * size)
    for j in range(0, size, 2):
        c0, r0 = j // 8, j % 8
        for t in tables:
            head = t[c0]
            row0 = jnp.broadcast_to(head[r0 : r0 + 1, :], wide)
            row1 = jnp.broadcast_to(head[r0 + 1 : r0 + 2, :], wide)
            a = jnp.broadcast_to(row0[:, j : j + 1], wide)
            b = jnp.broadcast_to(row1[:, j : j + 1], wide)
            c = jnp.broadcast_to(row1[:, j + 1 : j + 2], wide)
            inv = 1.0 / a
            ratio = b * inv
            inv1 = 1.0 / (c - ratio * b)
            lifted = row1 - ratio * row0
            scaled0 = row0 * inv
            scaled1 = lifted * inv1
            for k in range(c0, rows):
                col0 = jnp.broadcast_to(t[k][:, j : j + 1], wide)
                col1 = jnp.broadcast_to(t[k][:, j + 1 : j + 2], wide) - ratio * col0
                if k == c0:
                    col0 = jnp.where(sub > r0, col0, 0.0)
                    col1 = jnp.where(sub > r0 + 1, col1, 0.0)
                t[k] = t[k] - col0 * scaled0 - col1 * scaled1
    out = []
    for t in tables:
        joined = jnp.concatenate(t, axis=0)
        diag = jnp.sum(joined[:, :size] * eye, axis=1, keepdims=True)
        out.append(joined[:, size:] * lax.rsqrt(diag))
    return out


def split3(value):
    high = value.astype(BF16)
    rest = value - high.astype(F32)
    mid = rest.astype(BF16)
    return high, mid, (rest - mid.astype(F32)).astype(BF16)


def tail_kernel(
    where_ref, pairing_ref, near_ref, far_ref,
    out_up, out_low, moved, loose, gram_ref, table, *, half_rows, units
):
    order, rank = moved.shape
    sides = order // BLOCK
    unit = order // units
    share = out_up.shape[0]

    for k in range(sides):
        loose[k * BLOCK : (k + 1) * BLOCK, :] = far_ref[:, k * rank : (k + 1) * rank].astype(F32)

    @pl.loop(0, units)
    def _(i):
        moved[pl.ds(pl.multiple_of(pairing_ref[i] * unit, unit), unit), :] = loose[
            pl.ds(pl.multiple_of(i * unit, unit), unit), :
        ]

    swapped = moved[...].astype(BF16)
    third_right = jnp.concatenate(
        [
            jnp.dot(
                near_ref[:, k * order : (k + 1) * order], swapped, preferred_element_type=F32
            ).astype(BF16)
            for k in range(sides)
        ],
        axis=0,
    )
    left = sides * rank
    loose[...] = sum(
        contract(
            near_ref[:, k * order : (k + 1) * order],
            far_ref[:, left + k * rank : left + (k + 1) * rank],
        )
        for k in range(sides)
    )

    @pl.loop(0, units)
    def _(i):
        moved[pl.ds(pl.multiple_of(i * unit, unit), unit), :] = loose[
            pl.ds(pl.multiple_of(pairing_ref[i] * unit, unit), unit), :
        ]

    thirds = (third_right, moved[...].astype(BF16))
    for s, (third, square_ref) in enumerate(zip(thirds, (near_ref, far_ref))):
        base = (sides * order, 2 * left)[s]
        parts = [None] * (order // BLOCK)
        for k in range(order // BLOCK):
            width = order - k * BLOCK
            strip = square_ref[:, base : base + width]
            base += width
            term = jnp.dot(strip, third[k * BLOCK :], preferred_element_type=F32)
            parts[k] = term if parts[k] is None else parts[k] + term
            if width > BLOCK:
                below = lax.dot_general(
                    strip[:, BLOCK:],
                    third[k * BLOCK : (k + 1) * BLOCK],
                    (((0,), (0,)), ((), ())),
                    preferred_element_type=F32,
                )
                for m in range(k + 1, order // BLOCK):
                    piece = below[(m - k - 1) * BLOCK : (m - k) * BLOCK]
                    parts[m] = piece if parts[m] is None else parts[m] + piece
        for k in range(order // BLOCK):
            table[s, k * BLOCK : (k + 1) * BLOCK, :] = parts[k]
        product = table[s]
        pieces = contract(third, jnp.concatenate(split3(product), axis=1))
        gram = (
            pieces[:, :rank] + pieces[:, rank : 2 * rank] + pieces[:, 2 * rank :]
        ) * (1.0 / half_rows)
        gram_ref[s, :, :rank] = gram
        gram_ref[s, :, rank:] = (
            lax.broadcasted_iota(jnp.int32, (rank, rank), 0)
            == lax.broadcasted_iota(jnp.int32, (rank, rank), 1)
        ).astype(F32)

    @pl.loop(0, rank // PIVOTS)
    def _(k):
        at = pl.multiple_of(k * PIVOTS, PIVOTS)
        rows = [gram_ref[s, pl.ds(at, PIVOTS), :] for s in range(2)]
        turned = [pltpu.roll(r[:, :rank], rank - at, 1)[:, :PIVOTS] for r in rows]
        inverses = inverse_factors(turned)
        beyond = lax.broadcasted_iota(jnp.int32, (PIVOTS, rank), 1) >= at + PIVOTS
        for s in range(2):
            done = dot_exact(inverses[s], rows[s])
            ahead = jnp.where(beyond, done[:, :rank], 0.0)
            gram_ref[s, :, :] = gram_ref[s, :, :] - dot_exact(ahead, done, ((0,), (0,)))
            gram_ref[s, pl.ds(at, PIVOTS), :] = done

    at = pl.multiple_of(where_ref[0] * share, share)
    for s, out in enumerate((out_up, out_low)):
        out[...] = dot_exact(
            table[s, pl.ds(at, share), :], gram_ref[s, :, rank:], ((1,), (1,))
        )


def tail(me, pairing, near, far, order, rank, half_rows, count):
    share = jax.ShapeDtypeStruct((order // count, rank), F32)
    smem = pl.BlockSpec(memory_space=pltpu.SMEM)
    vmem = pl.BlockSpec(memory_space=pltpu.VMEM)
    return pl.pallas_call(
        functools.partial(tail_kernel, half_rows=half_rows, units=count),
        out_shape=(share, share),
        in_specs=[smem, smem, vmem, vmem],
        out_specs=(vmem, vmem),
        scratch_shapes=[
            pltpu.VMEM((order, rank), F32),
            pltpu.VMEM((order, rank), F32),
            pltpu.VMEM((2, rank, 2 * rank), F32),
            pltpu.VMEM((2, order, rank), F32),
        ],
        compiler_params=pltpu.CompilerParams(vmem_limit_bytes=48 * 2**20),
    )(me[None], pairing, near, far)


def per_device(
    upper_left, upper_right, lower_left, lower_right, sketch_right, sketch_left, pairing
):
    count = lax.axis_size("cols")
    me = lax.axis_index("cols").astype(jnp.int32)
    half_rows = upper_left.shape[0] * count
    order, rank = upper_left.shape[1], sketch_right.shape[1]
    bits = list(range(count.bit_length() - 1))
    near_first = bits
    far_first = bits[:1] + bits[2:3] + bits[1:2] + bits[3:]
    near = jnp.concatenate(strips(upper_right, lower_right) + upper_strips(upper_left), axis=1)
    far = jnp.concatenate(
        strips(lower_left, sketch_right)
        + strips(upper_left, sketch_left)
        + upper_strips(lower_left),
        axis=1,
    )
    near, far = sum_rows([near, far], [near_first, far_first], me, count)
    return tail(me, pairing, near, far, order, rank, half_rows, count)


def solution(mesh):
    rows = P(("groups", "cols"), None)
    return jax.shard_map(
        per_device,
        mesh=mesh,
        in_specs=(rows,) * 6 + (P("groups"),),
        out_specs=(rows, rows),
        check_vma=False,
    )
```
